32 devices in a mesh: groups: 2 (over y), blk: 4 (over x, core), sub: 4 (over z).
Axes of the slice: x: 2, y: 2, z: 4, core: 2. Of those that a mesh axis runs over, the one named last changes fastest.
Arguments:
- velocity: float32 [2, 512, 1024], P(None, ('groups', 'blk', 'sub')), parts along dimension 1, may hold values from -6 to 6
- stress: float32 [3, 512, 1024], P(None, ('groups', 'blk', 'sub')), parts along dimension 1, may hold values from -6 to 6
- ice_mass: float32 [512, 1024], P(('groups', 'blk', 'sub')), parts along dimension 0, may hold values from 0.5 to 3
- strength: float32 [512, 1024], P(('groups', 'blk', 'sub')), parts along dimension 0, may hold values from 0.3 to 3
- coriolis: float32 [512, 1024], P(('groups', 'blk', 'sub')), parts along dimension 0, may hold values from -1.5 to 1.5
- air_stress: float32 [2, 512, 1024], P(None, ('groups', 'blk', 'sub')), parts along dimension 1, may hold values from -4 to 4
- ocean_current: float32 [1536, 2, 1024], P(('groups', 'blk', 'sub')), parts along dimension 0, may hold values from -6 to 6
- neighbours: int32 [512, 4], P(('groups', 'blk', 'sub')), parts along dimension 0, may hold values from -1 to 255, as said below
- ocean_tile: int32 [512], P(('groups', 'blk', 'sub')), parts along dimension 0, may hold values from 0 to 767, as said below
Outputs:
- velocity_out: float32 [2, 512, 1024], P(None, ('groups', 'blk', 'sub')), parts along dimension 1
- stress_out: float32 [3, 512, 1024], P(None, ('groups', 'blk', 'sub')), parts along dimension 1
The draws below stay inside these ranges and needn't reach their ends.
There are 2 independent parts, one for each index of `groups`. The reference program is written for one: setup_inputs(seed, part) draws one part's arguments, and reference() takes and returns one part's arrays. A program takes and returns all parts, laid end to end along the dimension named above; each array names one. Nothing has to cross between parts.
Inputs may be any that keep to these rules, and one draw needn't show every extreme that they name: Block b is held by device b // 16 in the order of blk+sub. The relation is symmetric: neighbours[b, 0] = a exactly when neighbours[a, 2] = b, and neighbours[b, 1] = a exactly when neighbours[a, 3] = b. The west and south neighbours of one device's blocks, counted together, lie on any one device at most 4 times, and so do their east and north neighbours; some device reaches 4. No block is its own neighbour. `ocean_tile`: no two blocks name the same tile. Tile t is held by device t // 48, which differs from the device holding the block only in its index along sub. One device's blocks name at most 8 tiles of any one device, and some device reaches 8.
All inputs are finite; a program needn't handle non-finite values.
Results may differ from the reference program's by a relative error of at most 0.00002.
Values sent between devices are 32-bit elements; how exact they have to be, the bound alone decides.
A program may use at most 64 MiB of HBM per device.

```python
import math
import jax
import jax.numpy as jnp
from jax import lax

SIDE = 32
CELLS = 1024
BLOCKS_DEV = 16
TILES_DEV = 48
ICE_BLOCKS = 256
OCEAN_TILES = 768
EDGE_CAP = 4
TILE_CAP = 8
SUBCYCLES = 8
N_SUB = 4


def draw_neighbours(key, part):
    key = jax.random.fold_in(key, 11)
    subkeys = jax.random.split(key, 6)
    devices = ICE_BLOCKS // BLOCKS_DEV
    groups = 2 * BLOCKS_DEV // EDGE_CAP
    offsets = jax.random.permutation(subkeys[0], devices - 1)[:groups] + 1
    grouping = jax.random.permutation(subkeys[1], 2 * BLOCKS_DEV) // EDGE_CAP
    entry_offset = offsets[grouping].reshape(BLOCKS_DEV, 2)
    entry_group = grouping.reshape(BLOCKS_DEV, 2)
    block_ids = jnp.arange(ICE_BLOCKS, dtype=jnp.int32)
    device_of = block_ids // BLOCKS_DEV
    slot_of = block_ids % BLOCKS_DEV
    outward = []
    for column in range(2):
        shuffle = jax.random.permutation(subkeys[2 + column], BLOCKS_DEV)
        partner = (device_of + entry_offset[slot_of, column]) % devices * BLOCKS_DEV + shuffle[slot_of]
        kept_link = jnp.logical_or(jax.random.randint(subkeys[4 + column], (ICE_BLOCKS,), 0, 8) > 0, entry_group[slot_of, column] == 0)
        forward = jnp.where(kept_link, partner, -1)
        backward = jnp.full((ICE_BLOCKS,), -1, jnp.int32).at[partner].set(jnp.where(kept_link, block_ids, -1))
        outward.append((forward, backward))
    return jnp.stack([outward[0][0], outward[1][0], outward[0][1], outward[1][1]], axis=1).astype(jnp.int32)


def draw_ocean_tile(key, part):
    key = jax.random.fold_in(key, 23)
    subkeys = jax.random.split(key, 4)
    devices = ICE_BLOCKS // BLOCKS_DEV
    groups = BLOCKS_DEV // TILE_CAP
    shifts = jax.random.permutation(subkeys[0], N_SUB)[:groups]
    slot_shift = shifts[jax.random.permutation(subkeys[1], BLOCKS_DEV) // TILE_CAP]
    block_ids = jnp.arange(ICE_BLOCKS, dtype=jnp.int32)
    device_of = block_ids // BLOCKS_DEV
    slot_of = block_ids % BLOCKS_DEV
    owner = device_of // N_SUB * N_SUB + (device_of % N_SUB + slot_shift[slot_of]) % N_SUB
    scores = jax.random.randint(subkeys[2], (devices, BLOCKS_DEV), 0, 1 << 20) * BLOCKS_DEV + jnp.arange(BLOCKS_DEV, dtype=jnp.int32)[None, :]
    ordering = jnp.argsort(scores, axis=1).astype(jnp.int32)
    jitter = jax.random.randint(subkeys[3], (devices, BLOCKS_DEV), 0, 3)
    jitter = jnp.where(ordering == BLOCKS_DEV - 1, 2, jnp.where(ordering == 0, 0, jitter))
    local_tile = 3 * ordering + jitter
    return (owner * TILES_DEV + local_tile[owner, slot_of]).astype(jnp.int32)


def level_of(key, shape, shards, smallest, largest):
    level = 1.0
    for dim, parts in shards:
        heights = jax.random.uniform(jax.random.fold_in(jax.random.fold_in(key, 6), dim), (parts,), jnp.float32, smallest / len(shards), largest / len(shards))
        level = level * jnp.repeat(jnp.exp(heights), shape[dim] // parts).reshape((-1,) + (1,) * (len(shape) - 1 - dim))
    return level


def bell_draw(key, dims, deviation, most, pieces=(), kind=jnp.bfloat16):
    array = deviation * jax.random.normal(key, dims, jnp.float32)
    if pieces:
        array = array * level_of(key, dims, pieces, -0.22, 0.18)
    return jnp.clip(array, -most, most).astype(kind)


def setup_inputs(seed: int = 0, part: int = 0) -> dict:
    key_of = jax.random.split(jax.random.key(seed), 10)
    own_keys = jax.random.split(jax.random.fold_in(key_of[9], part), 10)
    return {
        "velocity": bell_draw(own_keys[0], (2, ICE_BLOCKS, CELLS), 1.0, 6.0, ((1, 16),), jnp.float32),
        "stress": bell_draw(own_keys[1], (3, ICE_BLOCKS, CELLS), 1.0, 6.0, ((1, 16),), jnp.float32),
        "ice_mass": jnp.clip(jnp.exp(math.log(3.0) - 1.7917595 * jax.random.uniform(own_keys[2], (ICE_BLOCKS, CELLS), jnp.float32) ** level_of(own_keys[2], (ICE_BLOCKS, CELLS), ((0, 16),), -0.2, 0.2)), 0.5, 3.0),
        "strength": jnp.clip(jnp.exp(math.log(3.0) - 2.3025851 * jax.random.uniform(own_keys[3], (ICE_BLOCKS, CELLS), jnp.float32) ** level_of(own_keys[3], (ICE_BLOCKS, CELLS), ((0, 16),), -0.2, 0.2)), 0.3, 3.0),
        "coriolis": jnp.clip(jax.random.uniform(own_keys[4], (ICE_BLOCKS, CELLS), jnp.float32, -1.5, 1.5) * level_of(own_keys[4], (ICE_BLOCKS, CELLS), ((0, 16),), -0.4, 0.0), -1.5, 1.5),
        "air_stress": bell_draw(own_keys[5], (2, ICE_BLOCKS, CELLS), 0.5, 4.0, ((1, 16),), jnp.float32),
        "ocean_current": bell_draw(own_keys[6], (OCEAN_TILES, 2, CELLS), 1.0, 6.0, ((0, 16),), jnp.float32),
        "neighbours": draw_neighbours(jax.random.fold_in(jax.random.fold_in(key_of[9], part), 71), part),
        "ocean_tile": draw_ocean_tile(jax.random.fold_in(jax.random.fold_in(key_of[9], part), 71), part),
    }


ECC_SQUARE = 4.0
DELTA_FLOOR = 0.01
RELAX = 0.3
TIME_STEP = 0.5
SPEED_FLOOR = 0.01

def from_east(values, border):
    column = lax.broadcasted_iota(jnp.int32, values.shape, 2) % SIDE
    shifted = jnp.concatenate([values[..., 1:], jnp.zeros_like(values[..., :1])], axis=2)
    return jnp.where(column == SIDE - 1, jnp.repeat(border, SIDE, axis=2), shifted)

def from_west(values, border):
    column = lax.broadcasted_iota(jnp.int32, values.shape, 2) % SIDE
    shifted = jnp.concatenate([jnp.zeros_like(values[..., :1]), values[..., :-1]], axis=2)
    return jnp.where(column == 0, jnp.repeat(border, SIDE, axis=2), shifted)

def from_north(values, border):
    return jnp.concatenate([values[..., SIDE:], border], axis=2)

def from_south(values, border):
    return jnp.concatenate([border, values[..., :-SIDE]], axis=2)

def update_stress(velocity, stress, border_east, border_north, strength):
    eastern = from_east(velocity, border_east)
    northern = from_north(velocity, border_north)
    along_x = eastern[0] - velocity[0]
    across_x = eastern[1] - velocity[1]
    across_y = northern[0] - velocity[0]
    along_y = northern[1] - velocity[1]
    diverge = along_x + along_y
    tension = along_x - along_y
    shearing = across_y + across_x
    delta = jnp.sqrt(diverge * diverge + (tension * tension + shearing * shearing) / ECC_SQUARE + DELTA_FLOOR)
    viscous = strength / delta
    target = jnp.stack([viscous * diverge - strength, viscous * tension / ECC_SQUARE, viscous * shearing / ECC_SQUARE])
    return stress + RELAX * (target - stress)

def update_velocity(velocity, stress, border_west, border_south, ice_mass, coriolis, air_stress, current):
    western = from_west(stress, border_west)
    southern = from_south(stress, border_south)
    normal_xx = 0.5 * (stress[0] + stress[1])
    normal_yy = 0.5 * (stress[0] - stress[1])
    shear_xy = 0.5 * stress[2]
    west_xx = 0.5 * (western[0] + western[1])
    west_xy = 0.5 * western[2]
    south_yy = 0.5 * (southern[0] - southern[1])
    south_xy = 0.5 * southern[2]
    force_x = normal_xx - west_xx + shear_xy - south_xy
    force_y = shear_xy - west_xy + normal_yy - south_yy
    slip_x = current[0] - velocity[0]
    slip_y = current[1] - velocity[1]
    relative = jnp.sqrt(slip_x * slip_x + slip_y * slip_y + SPEED_FLOOR)
    inertia = ice_mass / TIME_STEP
    diagonal = inertia + relative
    turning = ice_mass * coriolis
    drive_x = inertia * velocity[0] + force_x + air_stress[0] + relative * current[0] - turning * current[1]
    drive_y = inertia * velocity[1] + force_y + air_stress[1] + relative * current[1] + turning * current[0]
    determinant = diagonal * diagonal + turning * turning
    return jnp.stack([(diagonal * drive_x + turning * drive_y) / determinant, (diagonal * drive_y - turning * drive_x) / determinant])

def pick_edges(edges, index):
    found = jnp.take(edges, jnp.maximum(index, 0), axis=1)
    return jnp.where((index >= 0)[None, :, None], found, jnp.zeros_like(found))

def reference(velocity, stress, ice_mass, strength, coriolis, air_stress, ocean_current, neighbours, ocean_tile):
    blocks = velocity.shape[1]
    current_rows = jnp.take(ocean_current, ocean_tile, axis=0)
    current = jnp.stack([current_rows[:, 0], current_rows[:, 1]])
    for substep in range(SUBCYCLES):
        square = velocity.reshape(2, blocks, SIDE, SIDE)
        border_east = pick_edges(square[..., 0], neighbours[:, 2])
        border_north = pick_edges(square[..., 0, :], neighbours[:, 3])
        stress = update_stress(velocity, stress, border_east, border_north, strength)
        square = stress.reshape(3, blocks, SIDE, SIDE)
        border_west = pick_edges(square[..., SIDE - 1], neighbours[:, 0])
        border_south = pick_edges(square[..., SIDE - 1, :], neighbours[:, 1])
        velocity = update_velocity(velocity, stress, border_west, border_south, ice_mass, coriolis, air_stress, current)
    return (velocity, stress)
```

```python
import functools

import jax
import jax.numpy as jnp
from jax import lax
from jax.experimental import pallas as pl
from jax.experimental.pallas import tpu as pltpu
from jax.sharding import PartitionSpec as P

SIDE = 32
SUBCYCLES = 8
LANES = 128
CHUNKS = 8

DELTA_FLOOR = 0.01
RELAX = 0.3
SPEED_FLOOR = 0.01
MESH = pl.DeviceIdType.MESH
F32 = jnp.float32


def roll(x, shift):
    shift = shift % LANES
    return x if shift == 0 else pltpu.roll(x, shift, 1)


def lanes_like(x):
    return lax.broadcasted_iota(jnp.int32, x.shape, 1)


def gather_edges(col_a, col_b, row_a, row_b, col_lane, row_lane):
    lane = lanes_like(row_a)
    inner = lane % SIDE
    quarter = lane // SIDE
    out = jnp.zeros_like(row_a)
    for base, chunks in ((0, col_a), (8, col_b)):
        for k in range(CHUNKS):
            out = jnp.where(inner == base + k, roll(chunks[k], base + k - col_lane), out)
    for base, row in ((16, row_a), (24, row_b)):
        for c in range(4):
            there = (quarter == c) & (inner >= base) & (inner < base + 8)
            out = jnp.where(there, roll(row, 24 * c + base - row_lane), out)
    return out


def column_to(edges, base, k, col_lane):
    return roll(edges, col_lane - base - k)


def row_to(edges, base, row_lane):
    lane = lanes_like(edges)
    out = roll(edges, row_lane - base)
    for c in range(1, 4):
        moved = roll(edges, row_lane - base - 24 * c)
        out = jnp.where(lane >= row_lane + 8 * c, moved, out)
    return out


def chunk(k):
    return pl.ds(LANES * k, LANES)


def repeat(start, stop, body):
    if stop - start <= 64:
        for i in range(start, stop):
            body(i)
    else:

        def step(i, carry):
            body(i)
            return carry

        lax.fori_loop(start, stop, step, 0)


def kernel(
    sizes,
    plan,
    requests,
    vel_in,
    stress_in,
    mass,
    strength,
    coriolis,
    air,
    ocean,
    vel,
    stress,
    edges,
    borders,
    v_pack,
    v_recv,
    s_pack,
    s_recv,
    asked,
    asked_s,
    ans_pack,
    ans_recv,
    cur,
    consts,
    v_send_sem,
    v_recv_sem,
    s_send_sem,
    s_recv_sem,
    q_send_sem,
    q_recv_sem,
    a_send_sem,
    a_recv_sem,
    local_sem,
):
    n, owners, cap, tcap, blocks = sizes
    group, blk, sub = lax.axis_index("groups"), lax.axis_index("blk"), lax.axis_index("sub")
    me = blk * owners + sub

    def peer(o):
        d = lax.rem(me + o, n)
        return (group, d // owners, lax.rem(d, owners))

    def sub_peer(o):
        return (group, blk, lax.rem(sub + o + owners, owners))

    barrier = pltpu.get_barrier_semaphore()
    repeat(1, n, lambda o: pl.semaphore_signal(barrier, inc=1, device_id=peer(o), device_id_type=MESH))
    pl.semaphore_wait(barrier, n - 1)

    def request_copy(o):
        return pltpu.make_async_remote_copy(
            src_ref=requests.at[o],
            dst_ref=asked.at[o],
            send_sem=q_send_sem.at[o],
            recv_sem=q_recv_sem.at[o],
            device_id=sub_peer(o),
            device_id_type=MESH,
        )

    def answer_copy(o):
        return pltpu.make_async_remote_copy(
            src_ref=ans_pack.at[pl.ds(o * tcap, tcap)],
            dst_ref=ans_recv.at[pl.ds(o * tcap, tcap)],
            send_sem=a_send_sem.at[o],
            recv_sem=a_recv_sem.at[o],
            device_id=sub_peer(-o),
            device_id_type=MESH,
        )

    for o in range(1, owners):
        request_copy(o).start()

    slots = n * cap
    v_src, s_src, v_land, s_land, t_land = 0, slots, 2 * slots, 2 * slots + 2 * blocks, 2 * slots + 4 * blocks
    remote = pl.ds(cap, slots - cap)

    def trade(first, pack, recv, send_sem, recv_sem):
        def fill(s):
            pack[s] = edges[pl.ds(plan[first + s], 1), :]

        def fill_own(s):
            recv[s] = edges[pl.ds(plan[first + s], 1), :]

        repeat(0, cap, fill_own)
        repeat(cap, slots, fill)

        def send(o):
            where = pl.ds(o * cap, cap)
            pltpu.make_async_remote_copy(
                src_ref=pack.at[where],
                dst_ref=recv.at[where],
                send_sem=send_sem,
                recv_sem=recv_sem,
                device_id=peer(o),
                device_id_type=MESH,
            ).start()

        repeat(1, n, send)

    def wait_all(ref, sem):
        pltpu.make_async_copy(ref.at[remote], ref.at[remote], sem).wait()

    def land(first, recv):
        for b in range(blocks):
            from_col = recv[plan[first + 2 * b]]
            from_row = recv[plan[first + 2 * b + 1]]
            inner = lanes_like(from_col) % SIDE
            borders[pl.ds(b, 1), :] = jnp.where(inner < 16, from_col, from_row)
        return borders[...]

    def send_velocity(u, v):
        edges[...] = gather_edges(u, v, u[0], v[0], 0, 0)
        trade(v_src, v_pack, v_recv, v_send_sem, v_recv_sem)

    def stress_step(source):
        u = [vel_in[0, :, chunk(k)] if source else vel[0, :, chunk(k)] for k in range(CHUNKS)]
        v = [vel_in[1, :, chunk(k)] if source else vel[1, :, chunk(k)] for k in range(CHUNKS)]
        old = stress_in if source else stress
        wait_all(v_recv, v_recv_sem)
        got = land(v_land, v_recv)
        lane = lanes_like(got)
        inner = lane % SIDE
        ru = [roll(x, -SIDE) for x in u] + [row_to(got, 16, 96)]
        rv = [roll(x, -SIDE) for x in v] + [row_to(got, 24, 96)]
        xx, yy, xy = [], [], []
        for k in range(CHUNKS):
            u_e = jnp.where(inner == 31, column_to(got, 0, k, 31), roll(u[k], -1))
            v_e = jnp.where(inner == 31, column_to(got, 8, k, 31), roll(v[k], -1))
            u_n = jnp.where(lane < 96, ru[k], ru[k + 1])
            v_n = jnp.where(lane < 96, rv[k], rv[k + 1])
            along_x, along_y = u_e - u[k], v_n - v[k]
            diverge = along_x + along_y
            tension = along_x - along_y
            shearing = (u_n - u[k]) + (v_e - v[k])
            square = diverge * diverge + 0.25 * (tension * tension + shearing * shearing) + DELTA_FLOOR
            p = strength[:, chunk(k)]
            viscous = p * lax.rsqrt(square)
            s1, s2, s12 = (old[c, :, chunk(k)] for c in range(3))
            s1 = s1 + RELAX * (viscous * diverge - p - s1)
            s2 = s2 + RELAX * (0.25 * viscous * tension - s2)
            s12 = s12 + RELAX * (0.25 * viscous * shearing - s12)
            stress[0, :, chunk(k)] = s1
            stress[1, :, chunk(k)] = s2
            stress[2, :, chunk(k)] = s12
            xx.append(0.5 * (s1 + s2))
            yy.append(0.5 * (s1 - s2))
            xy.append(0.5 * s12)
        wait_all(v_pack, v_send_sem)
        edges[...] = gather_edges(xx, xy, yy[-1], xy[-1], 31, 96)
        trade(s_src, s_pack, s_recv, s_send_sem, s_recv_sem)

    def velocity_step(source, more):
        wait_all(s_recv, s_recv_sem)
        got = land(s_land, s_recv)
        lane = lanes_like(got)
        inner = lane % SIDE
        old_yy, old_xy = row_to(got, 16, 0), row_to(got, 24, 0)
        us, vs = [], []
        for k in range(CHUNKS):
            s1, s2, s12 = (stress[c, :, chunk(k)] for c in range(3))
            xx, yy, xy = 0.5 * (s1 + s2), 0.5 * (s1 - s2), 0.5 * s12
            xx_w = jnp.where(inner == 0, column_to(got, 0, k, 0), roll(xx, 1))
            xy_w = jnp.where(inner == 0, column_to(got, 8, k, 0), roll(xy, 1))
            new_yy, new_xy = roll(yy, SIDE), roll(xy, SIDE)
            yy_s = jnp.where(lane < SIDE, old_yy, new_yy)
            xy_s = jnp.where(lane < SIDE, old_xy, new_xy)
            old_yy, old_xy = new_yy, new_xy
            force_x = xx - xx_w + xy - xy_s
            force_y = xy - xy_w + yy - yy_s
            here = vel_in if source else vel
            u, v = here[0, :, chunk(k)], here[1, :, chunk(k)]
            uo, vo = cur[0, :, chunk(k)], cur[1, :, chunk(k)]
            inertia, r, cx, cy = (consts[c, :, chunk(k)] for c in range(4))
            dx, dy = uo - u, vo - v
            drag = jnp.sqrt(dx * dx + dy * dy + SPEED_FLOOR)
            a = inertia + drag
            gx = inertia * u + force_x + cx + drag * uo
            gy = inertia * v + force_y + cy + drag * vo
            inv = 1.0 / (a * a + r * r)
            u, v = (a * gx + r * gy) * inv, (a * gy - r * gx) * inv
            vel[0, :, chunk(k)] = u
            vel[1, :, chunk(k)] = v
            us.append(u)
            vs.append(v)
        wait_all(s_pack, s_send_sem)
        if more:
            send_velocity(us, vs)

    zero_row = jnp.zeros((1, LANES), F32)
    v_recv[slots] = zero_row
    s_recv[slots] = zero_row
    send_velocity(
        [vel_in[0, :, chunk(k)] for k in range(CHUNKS)], [vel_in[1, :, chunk(k)] for k in range(CHUNKS)]
    )

    asked[0] = requests[0]
    for o in range(1, owners):
        request_copy(o).wait()
    to_scalar = pltpu.make_async_copy(asked, asked_s, local_sem)
    to_scalar.start()
    to_scalar.wait()
    for o in range(owners):
        for t in range(tcap):
            (ans_pack if o else ans_recv)[o * tcap + t] = ocean[asked_s[o, 0, t]]
        if o:
            answer_copy(o).start()

    stress_step(True)

    for o in range(1, owners):
        answer_copy(o).wait()
    for b in range(blocks):
        row = ans_recv[plan[t_land + b]]
        cur[0, pl.ds(b, 1), :] = row[0:1]
        cur[1, pl.ds(b, 1), :] = row[1:2]
    for k in range(CHUNKS):
        m = mass[:, chunk(k)]
        r = m * coriolis[:, chunk(k)]
        consts[0, :, chunk(k)] = 2.0 * m
        consts[1, :, chunk(k)] = r
        consts[2, :, chunk(k)] = air[0, :, chunk(k)] - r * cur[1, :, chunk(k)]
        consts[3, :, chunk(k)] = air[1, :, chunk(k)] + r * cur[0, :, chunk(k)]

    velocity_step(True, True)

    def subcycle(_, carry):
        stress_step(False)
        velocity_step(False, True)
        return carry

    lax.fori_loop(0, SUBCYCLES - 2, subcycle, 0)
    stress_step(False)
    velocity_step(False, False)


def make_plan(neighbours, ocean_tile, sizes, tiles_dev):
    n, owners, cap, tcap, blocks = sizes
    sub = lax.axis_index("sub")
    me = lax.axis_index("blk") * owners + sub
    entry = jnp.arange(2 * blocks, dtype=jnp.int32)

    def sending(targets):
        t = targets.reshape(-1)
        away = jnp.where(t >= 0, (t // blocks - me) % n, n)
        ahead = (away[:, None] == away[None, :]) & (entry[None, :] < entry[:, None])
        place = away * cap + jnp.sum(ahead.astype(jnp.int32), axis=1)
        slot = jnp.arange(n * cap, dtype=jnp.int32)
        hit = (place[None, :] == slot[:, None]) & (away < n)[None, :]
        return jnp.sum(jnp.where(hit, (entry // 2)[None, :], 0), axis=1)

    def landing(sources):
        s = sources.reshape(-1)
        known = s >= 0
        away = jnp.where(known, (me - s // blocks) % n, n)
        key = s * 2 + entry % 2
        ahead = (away[:, None] == away[None, :]) & (key[None, :] < key[:, None])
        place = away * cap + jnp.sum(ahead.astype(jnp.int32), axis=1)
        return jnp.where(known, place, n * cap)

    away = (ocean_tile // tiles_dev - sub) % owners
    order = jnp.arange(blocks, dtype=jnp.int32)
    ahead = (away[:, None] == away[None, :]) & (order[None, :] < order[:, None])
    rank = jnp.sum(ahead.astype(jnp.int32), axis=1)
    place = away * tcap + rank
    lane = jnp.arange(LANES, dtype=jnp.int32)
    wanted = away * LANES + rank
    spots = jnp.arange(owners, dtype=jnp.int32)[:, None] * LANES + lane[None, :]
    hit = spots[:, :, None] == wanted[None, None, :]
    requests = jnp.sum(jnp.where(hit, (ocean_tile % tiles_dev)[None, None, :], 0), axis=2)
    plan = jnp.concatenate(
        [
            sending(neighbours[:, 0:2]),
            sending(neighbours[:, 2:4]),
            landing(neighbours[:, 2:4]),
            landing(neighbours[:, 0:2]),
            place,
        ]
    )
    return plan, requests.reshape(owners, 1, LANES)


def shards(
    velocity, stress, ice_mass, strength, coriolis, air_stress, ocean_current, neighbours, ocean_tile
):
    blocks = velocity.shape[1]
    n = lax.axis_size(("blk", "sub"))
    owners = lax.axis_size("sub")
    cap = max(2, 4 * blocks // n)
    tcap = max(1, 2 * blocks // owners)
    sizes = (n, owners, cap, tcap, blocks)
    cells = velocity.shape[2]
    plan, requests = make_plan(neighbours, ocean_tile, sizes, ocean_current.shape[0])
    slots = n * cap
    vmem = pl.BlockSpec(memory_space=pltpu.VMEM)
    dma = pltpu.SemaphoreType.DMA
    return pl.pallas_call(
        functools.partial(kernel, sizes),
        out_shape=(
            jax.ShapeDtypeStruct(velocity.shape, F32),
            jax.ShapeDtypeStruct(stress.shape, F32),
        ),
        in_specs=[pl.BlockSpec(memory_space=pltpu.SMEM)] + [vmem] * 8,
        out_specs=(vmem, vmem),
        scratch_shapes=[
            pltpu.VMEM((blocks, LANES), F32),
            pltpu.VMEM((blocks, LANES), F32),
            pltpu.VMEM((slots, 1, LANES), F32),
            pltpu.VMEM((slots + 1, 1, LANES), F32),
            pltpu.VMEM((slots, 1, LANES), F32),
            pltpu.VMEM((slots + 1, 1, LANES), F32),
            pltpu.VMEM((owners, 1, LANES), jnp.int32),
            pltpu.SMEM((owners, 1, LANES), jnp.int32),
            pltpu.VMEM((owners * tcap, 2, cells), F32),
            pltpu.VMEM((owners * tcap, 2, cells), F32),
            pltpu.VMEM((2, blocks, cells), F32),
            pltpu.VMEM((4, blocks, cells), F32),
            dma,
            dma,
            dma,
            dma,
            dma((owners,)),
            dma((owners,)),
            dma((owners,)),
            dma((owners,)),
            dma,
        ],
        compiler_params=pltpu.CompilerParams(collective_id=0, has_side_effects=True),
    )(plan, requests, velocity, stress, ice_mass, strength, coriolis, air_stress, ocean_current)


def solution(mesh):
    split = ("groups", "blk", "sub")
    placed = (
        P(None, split, None),
        P(None, split, None),
        P(split, None),
        P(split, None),
        P(split, None),
        P(None, split, None),
        P(split, None, None),
        P(split, None),
        P(split),
    )
    return jax.shard_map(
        shards,
        mesh=mesh,
        in_specs=placed,
        out_specs=(P(None, split, None), P(None, split, None)),
        check_vma=False,
    )
```

```python
import functools

import jax
import jax.numpy as jnp
from jax import lax
from jax.experimental import pallas as pl
from jax.experimental.pallas import tpu as pltpu
from jax.sharding import PartitionSpec as P

SIDE = 32
SUBCYCLES = 8
LANES = 128
CHUNKS = 8

DELTA_FLOOR = 0.01
RELAX = 0.3
SPEED_FLOOR = 0.01
MESH = pl.DeviceIdType.MESH
F32 = jnp.float32


def roll(x, shift):
    shift = shift % LANES
    return x if shift == 0 else pltpu.roll(x, shift, 1)


def lanes_like(x):
    return lax.broadcasted_iota(jnp.int32, x.shape, 1)


def gather_edges(col_a, col_b, row_a, row_b, col_lane, row_lane):
    lane = lanes_like(row_a)
    inner = lane % SIDE
    quarter = lane // SIDE
    out = jnp.zeros_like(row_a)
    for base, chunks in ((0, col_a), (8, col_b)):
        for k in range(CHUNKS):
            out = jnp.where(inner == base + k, roll(chunks[k], base + k - col_lane), out)
    for base, row in ((16, row_a), (24, row_b)):
        for c in range(4):
            there = (quarter == c) & (inner >= base) & (inner < base + 8)
            out = jnp.where(there, roll(row, 24 * c + base - row_lane), out)
    return out


def column_to(edges, base, k, col_lane):
    return roll(edges, col_lane - base - k)


def row_to(edges, base, row_lane):
    lane = lanes_like(edges)
    out = roll(edges, row_lane - base)
    for c in range(1, 4):
        moved = roll(edges, row_lane - base - 24 * c)
        out = jnp.where(lane >= row_lane + 8 * c, moved, out)
    return out


def chunk(k):
    return pl.ds(LANES * k, LANES)


def repeat(start, stop, body):
    if stop - start <= 64:
        for i in range(start, stop):
            body(i)
    else:

        def step(i, carry):
            body(i)
            return carry

        lax.fori_loop(start, stop, step, 0)


def kernel(
    sizes,
    plan,
    table_row,
    vel_in,
    stress_in,
    mass,
    strength,
    coriolis,
    air,
    ocean,
    vel,
    stress,
    low_edges,
    high_edges,
    near,
    far,
    corners,
    corner_lane,
    corner_slot,
    halo,
    pack,
    recv_even,
    recv_odd,
    h_pack,
    h_recv,
    table,
    table_s,
    ans_pack,
    ans_recv,
    cur,
    consts,
    send_sem,
    recv_sem,
    h_send_sem,
    h_recv_sem,
    t_send_sem,
    t_recv_sem,
    a_send_sem,
    a_recv_sem,
    local_sem,
):
    n, owners, cap, tcap, blocks = sizes
    rows = cap + 1
    slots = n * cap
    zero_slot = n * rows
    group, blk, sub = lax.axis_index("groups"), lax.axis_index("blk"), lax.axis_index("sub")
    me = blk * owners + sub
    recv = (recv_even, recv_odd)
    low_src, high_src = 0, slots
    land = 2 * slots
    h_land = land + 4 * blocks
    t_land = h_land + 2 * blocks

    def peer(o):
        d = lax.rem(me + o, n)
        return (group, d // owners, lax.rem(d, owners))

    def sub_peer(o):
        return (group, blk, lax.rem(sub + o + owners, owners))

    def send_to(o, source, target, sent, received, device):
        return pltpu.make_async_remote_copy(
            src_ref=source,
            dst_ref=target,
            send_sem=sent,
            recv_sem=received,
            device_id=device,
            device_id_type=MESH,
        )

    def wait_all(ref, sem):
        pltpu.make_async_copy(ref, ref, sem).wait()

    def answer_copy(o):
        where = pl.ds(o * tcap, tcap)
        return send_to(
            o, ans_pack.at[where], ans_recv.at[where], a_send_sem.at[o], a_recv_sem.at[o], sub_peer(-o)
        )

    barrier = pltpu.get_barrier_semaphore()
    repeat(1, n, lambda o: pl.semaphore_signal(barrier, inc=1, device_id=peer(o), device_id_type=MESH))
    pl.semaphore_wait(barrier, n - 1)
    repeat(
        1, n, lambda o: send_to(o, table_row, table.at[o], t_send_sem, t_recv_sem, peer(o)).start()
    )

    def trade(u, v, parity):
        lane = lanes_like(u[0])
        block = lax.broadcasted_iota(jnp.int32, u[0].shape, 0)
        low = gather_edges(u, v, u[0], v[0], 0, 0)
        high = gather_edges(u, v, u[-1], v[-1], 31, 96)
        low_edges[0:blocks] = low
        low_edges[blocks : 2 * blocks] = roll(low, -16)
        high_edges[0:blocks] = high
        high_edges[blocks : 2 * blocks] = roll(high, 16)
        spread = jnp.zeros_like(low)
        for place, value in enumerate((u[0][:, 31:32], v[0][:, 31:32], u[-1][:, 96:97], v[-1][:, 96:97])):
            spread = jnp.where(lane == block + place * blocks, value, spread)
        corner_row = jnp.sum(spread, axis=0, keepdims=True)
        half = lax.broadcasted_iota(jnp.int32, (1, LANES), 1) % SIDE < 16
        into = recv[parity]

        def fill(o, target):
            for t in range(cap):
                low_row = low_edges[pl.ds(plan[low_src + o * cap + t], 1), :]
                high_row = high_edges[pl.ds(plan[high_src + o * cap + t], 1), :]
                target[o * rows + t] = jnp.where(half, low_row, high_row)
            target[o * rows + cap] = corner_row

        def fill_and_send(o):
            fill(o, pack)
            where = pl.ds(o * rows, rows)
            send_to(
                o, pack.at[where], into.at[where], send_sem.at[parity], recv_sem.at[parity], peer(o)
            ).start()

        repeat(1, n, fill_and_send)
        fill(0, into)

    remote = pl.ds(rows, (n - 1) * rows)

    def arrive(parity):
        wait_all(recv[parity].at[remote], recv_sem.at[parity])
        half = lax.broadcasted_iota(jnp.int32, (1, LANES), 1) % SIDE < 16
        for b in range(blocks):
            east, north, west, south = (recv[parity][plan[land + 4 * b + c]] for c in range(4))
            near[pl.ds(b, 1), :] = jnp.where(half, east, south)
            far[pl.ds(b, 1), :] = jnp.where(half, north, west)
            corners[0, pl.ds(b, 1), :] = recv[parity][corner_slot[b]]
            corners[1, pl.ds(b, 1), :] = recv[parity][corner_slot[blocks + b]]
        straight, crossed = near[0:blocks], far[0:blocks]
        half = lanes_like(straight) % SIDE < 16
        low = jnp.where(half, straight, roll(crossed, 16))
        high = jnp.where(half, roll(crossed, -16), straight)
        return low, high

    def corner_value(which, place):
        x = corners[which]
        hit = lanes_like(x) == corner_lane[which] + place * blocks
        return jnp.sum(jnp.where(hit, x, 0.0), axis=1, keepdims=True)

    def advance(stress_old, u, v, u_e, v_e, u_n, v_n, p):
        along_x, along_y = u_e - u, v_n - v
        diverge = along_x + along_y
        tension = along_x - along_y
        shearing = (u_n - u) + (v_e - v)
        square = diverge * diverge + 0.25 * (tension * tension + shearing * shearing) + DELTA_FLOOR
        viscous = p * lax.rsqrt(square)
        s1, s2, s12 = stress_old
        return (
            s1 + RELAX * (viscous * diverge - p - s1),
            s2 + RELAX * (0.25 * viscous * tension - s2),
            s12 + RELAX * (0.25 * viscous * shearing - s12),
        )

    def halo_step(high):
        lane = lanes_like(high)
        inner = lane % SIDE
        column = inner < 16

        def ahead(x, north_west, south_east):
            up = jnp.where(lane < 96, roll(x, -32), roll(x, 95))
            up = jnp.where(lane == 103, north_west, up)
            right = jnp.where(inner == 23, roll(x, -25), roll(x, -1))
            right = jnp.where(lane == 119, south_east, right)
            return jnp.where(column, up, right)

        mine = low_edges[0:blocks]
        u, v = high, roll(high, -8)
        mine_u, mine_v = mine, roll(mine, -8)
        ahead_u = ahead(u, corner_value(0, 0), corner_value(1, 2))
        ahead_v = ahead(v, corner_value(0, 1), corner_value(1, 3))
        s1, s2, s12 = advance(
            (halo[0], halo[1], halo[2]),
            u,
            v,
            jnp.where(column, mine_u, ahead_u),
            jnp.where(column, mine_v, ahead_v),
            jnp.where(column, ahead_u, mine_u),
            jnp.where(column, ahead_v, mine_v),
            halo[3],
        )
        halo[0], halo[1], halo[2] = s1, s2, s12
        return 0.5 * (s1 + s2), 0.5 * (s1 - s2), 0.5 * s12

    def subcycle(parity, first, last):
        here, old = (vel_in, stress_in) if first else (vel, stress)
        low, high = arrive(parity)
        if first:
            settle()
        halo_xx, halo_yy, halo_xy = halo_step(high)
        lane = lanes_like(low)
        inner = lane % SIDE
        us = [here[0, :, chunk(k)] for k in range(CHUNKS)]
        vs = [here[1, :, chunk(k)] for k in range(CHUNKS)]
        old_yy, old_xy = row_to(halo_yy, 16, 0), row_to(halo_xy, 16, 0)
        next_u, next_v = roll(us[0], -SIDE), roll(vs[0], -SIDE)
        new_u, new_v = [], []
        for k in range(CHUNKS):
            u, v = us[k], vs[k]
            this_u, this_v = next_u, next_v
            if k + 1 < CHUNKS:
                next_u, next_v = roll(us[k + 1], -SIDE), roll(vs[k + 1], -SIDE)
            else:
                next_u, next_v = row_to(low, 16, 96), row_to(low, 24, 96)
            s1, s2, s12 = advance(
                [old[c, :, chunk(k)] for c in range(3)],
                u,
                v,
                jnp.where(inner == 31, column_to(low, 0, k, 31), roll(u, -1)),
                jnp.where(inner == 31, column_to(low, 8, k, 31), roll(v, -1)),
                jnp.where(lane < 96, this_u, next_u),
                jnp.where(lane < 96, this_v, next_v),
                strength[:, chunk(k)],
            )
            stress[0, :, chunk(k)] = s1
            stress[1, :, chunk(k)] = s2
            stress[2, :, chunk(k)] = s12
            xx, yy, xy = 0.5 * (s1 + s2), 0.5 * (s1 - s2), 0.5 * s12
            xx_w = jnp.where(inner == 0, column_to(halo_xx, 0, k, 0), roll(xx, 1))
            xy_w = jnp.where(inner == 0, column_to(halo_xy, 0, k, 0), roll(xy, 1))
            new_yy, new_xy = roll(yy, SIDE), roll(xy, SIDE)
            yy_s = jnp.where(lane < SIDE, old_yy, new_yy)
            xy_s = jnp.where(lane < SIDE, old_xy, new_xy)
            old_yy, old_xy = new_yy, new_xy
            force_x = xx - xx_w + xy - xy_s
            force_y = xy - xy_w + yy - yy_s
            uo, vo = cur[0, :, chunk(k)], cur[1, :, chunk(k)]
            inertia, r, cx, cy = (consts[c, :, chunk(k)] for c in range(4))
            dx, dy = uo - u, vo - v
            drag = jnp.sqrt(dx * dx + dy * dy + SPEED_FLOOR)
            a = inertia + drag
            gx = inertia * u + force_x + cx + drag * uo
            gy = inertia * v + force_y + cy + drag * vo
            inv = 1.0 / (a * a + r * r)
            u, v = (a * gx + r * gy) * inv, (a * gy - r * gx) * inv
            vel[0, :, chunk(k)] = u
            vel[1, :, chunk(k)] = v
            new_u.append(u)
            new_v.append(v)
        wait_all(pack.at[remote], send_sem.at[parity])
        if not last:
            trade(new_u, new_v, 1 - parity)

    def settle():
        wait_all(h_recv.at[pl.ds(2 * cap, 2 * (slots - cap))], h_recv_sem)
        wait_all(h_pack.at[pl.ds(2 * cap, 2 * (slots - cap))], h_send_sem)
        half = lax.broadcasted_iota(jnp.int32, (1, LANES), 1) % SIDE < 16
        for b in range(blocks):
            west, south = 2 * plan[h_land + 2 * b], 2 * plan[h_land + 2 * b + 1]
            near[pl.ds(b, 1), :] = jnp.where(half, h_recv[west], h_recv[south])
            far[pl.ds(b, 1), :] = jnp.where(half, h_recv[west + 1], h_recv[south + 1])
        first, second = near[0:blocks], far[0:blocks]
        halo[0], halo[1] = first, roll(first, -8)
        halo[2], halo[3] = second, roll(second, -8)
        for o in range(1, owners):
            answer_copy(o).wait()
        for b in range(blocks):
            row = ans_recv[plan[t_land + b]]
            cur[0, pl.ds(b, 1), :] = row[0:1]
            cur[1, pl.ds(b, 1), :] = row[1:2]
        for k in range(CHUNKS):
            m = mass[:, chunk(k)]
            r = m * coriolis[:, chunk(k)]
            consts[0, :, chunk(k)] = 2.0 * m
            consts[1, :, chunk(k)] = r
            consts[2, :, chunk(k)] = air[0, :, chunk(k)] - r * cur[1, :, chunk(k)]
            consts[3, :, chunk(k)] = air[1, :, chunk(k)] + r * cur[0, :, chunk(k)]

    zero_row = jnp.zeros((1, LANES), F32)
    recv_even[zero_slot] = zero_row
    recv_odd[zero_slot] = zero_row
    h_recv[2 * slots] = zero_row
    h_recv[2 * slots + 1] = zero_row
    trade([vel_in[0, :, chunk(k)] for k in range(CHUNKS)], [vel_in[1, :, chunk(k)] for k in range(CHUNKS)], 0)

    s1, s2, s12 = ([stress_in[c, :, chunk(k)] for k in range(CHUNKS)] for c in range(3))
    p = [strength[:, chunk(k)] for k in range(CHUNKS)]
    first = gather_edges(s1, s2, s1[-1], s2[-1], 31, 96)
    second = gather_edges(s12, p, s12[-1], p[-1], 31, 96)
    for copy in range(2):
        near[copy * blocks : (copy + 1) * blocks] = first
        far[copy * blocks : (copy + 1) * blocks] = second

    def fill_halo(o, target):
        for t in range(cap):
            s = plan[high_src + o * cap + t]
            target[2 * (o * cap + t)] = near[pl.ds(s, 1), :]
            target[2 * (o * cap + t) + 1] = far[pl.ds(s, 1), :]

    def send_halo(o):
        fill_halo(o, h_pack)
        where = pl.ds(2 * o * cap, 2 * cap)
        send_to(o, h_pack.at[where], h_recv.at[where], h_send_sem, h_recv_sem, peer(o)).start()

    repeat(1, n, send_halo)
    fill_halo(0, h_recv)

    table[0] = table_row[...]
    wait_all(table.at[pl.ds(1, n - 1)], t_recv_sem)
    wait_all(table.at[pl.ds(1, n - 1)], t_send_sem)
    to_scalar = pltpu.make_async_copy(table, table_s, local_sem)
    to_scalar.start()
    to_scalar.wait()
    for o in range(owners):
        holder = blk * owners + lax.rem(sub - o + owners, owners)
        slot = lax.rem(me - holder + n, n)
        for t in range(tcap):
            tile = ocean[table_s[slot, 0, 4 * blocks + o * tcap + t]]
            (ans_pack if o else ans_recv)[o * tcap + t] = tile
        if o:
            answer_copy(o).start()
    for b in range(blocks):
        for which in range(2):
            via = jnp.maximum(table_s[0, 0, 4 * b + which], 0)
            there = lax.rem(me - via // blocks + n, n)
            far_block = table_s[there, 0, 4 * lax.rem(via, blocks) + 3 - which]
            known = far_block >= 0
            far_block = jnp.maximum(far_block, 0)
            slot = lax.rem(me - far_block // blocks + n, n) * rows + cap
            corner_slot[which * blocks + b] = jnp.where(known, slot, zero_slot)
            corner_lane[which, pl.ds(b, 1), :] = jnp.full((1, LANES), lax.rem(far_block, blocks), jnp.int32)

    subcycle(0, True, False)

    def pair(_, carry):
        subcycle(1, False, False)
        subcycle(0, False, False)
        return carry

    lax.fori_loop(0, (SUBCYCLES - 2) // 2, pair, 0)
    subcycle(1, False, True)


def make_plan(neighbours, ocean_tile, sizes, tiles_dev):
    n, owners, cap, tcap, blocks = sizes
    sub = lax.axis_index("sub")
    me = lax.axis_index("blk") * owners + sub
    entry = jnp.arange(2 * blocks, dtype=jnp.int32)

    def sending(targets, content):
        t = targets.reshape(-1)
        away = jnp.where(t >= 0, (t // blocks - me) % n, n)
        ahead = (away[:, None] == away[None, :]) & (entry[None, :] < entry[:, None])
        place = away * cap + jnp.sum(ahead.astype(jnp.int32), axis=1)
        slot = jnp.arange(n * cap, dtype=jnp.int32)
        hit = (place[None, :] == slot[:, None]) & (away < n)[None, :]
        return jnp.sum(jnp.where(hit, content[None, :], 0), axis=1)

    def landing(sources):
        s = sources.reshape(-1)
        known = s >= 0
        away = jnp.where(known, (me - s // blocks) % n, n)
        key = s * 2 + entry % 2
        ahead = (away[:, None] == away[None, :]) & (key[None, :] < key[:, None])
        rank = jnp.sum(ahead.astype(jnp.int32), axis=1)
        main = jnp.where(known, away * (cap + 1) + rank, n * (cap + 1))
        return main.reshape(-1, 2), jnp.where(known, away * cap + rank, n * cap)

    away = (ocean_tile // tiles_dev - sub) % owners
    order = jnp.arange(blocks, dtype=jnp.int32)
    ahead = (away[:, None] == away[None, :]) & (order[None, :] < order[:, None])
    place = away * tcap + jnp.sum(ahead.astype(jnp.int32), axis=1)
    hit = jnp.arange(owners * tcap, dtype=jnp.int32)[:, None] == place[None, :]
    requests = jnp.sum(jnp.where(hit, (ocean_tile % tiles_dev)[None, :], 0), axis=1)
    row = jnp.concatenate([neighbours.reshape(-1), requests])
    row = jnp.pad(row, (0, LANES - row.shape[0])).reshape(1, LANES)
    from_east, _ = landing(neighbours[:, 2:4])
    from_west, halo_land = landing(neighbours[:, 0:2])
    kind = entry % 2
    plan = jnp.concatenate(
        [
            sending(neighbours[:, 0:2], entry // 2 + kind * blocks),
            sending(neighbours[:, 2:4], entry // 2 + (1 - kind) * blocks),
            jnp.concatenate([from_east, from_west], axis=1).reshape(-1),
            halo_land,
            place,
        ]
    )
    return plan, row


def shards(
    velocity, stress, ice_mass, strength, coriolis, air_stress, ocean_current, neighbours, ocean_tile
):
    blocks = velocity.shape[1]
    n = lax.axis_size(("blk", "sub"))
    owners = lax.axis_size("sub")
    cap = max(2, 4 * blocks // n)
    tcap = max(1, 2 * blocks // owners)
    sizes = (n, owners, cap, tcap, blocks)
    cells = velocity.shape[2]
    plan, row = make_plan(neighbours, ocean_tile, sizes, ocean_current.shape[0])
    slots = n * cap
    vmem = pl.BlockSpec(memory_space=pltpu.VMEM)
    dma = pltpu.SemaphoreType.DMA
    return pl.pallas_call(
        functools.partial(kernel, sizes),
        out_shape=(
            jax.ShapeDtypeStruct(velocity.shape, F32),
            jax.ShapeDtypeStruct(stress.shape, F32),
        ),
        in_specs=[pl.BlockSpec(memory_space=pltpu.SMEM)] + [vmem] * 8,
        out_specs=(vmem, vmem),
        scratch_shapes=[
            pltpu.VMEM((2 * blocks, LANES), F32),
            pltpu.VMEM((2 * blocks, LANES), F32),
            pltpu.VMEM((2 * blocks, LANES), F32),
            pltpu.VMEM((2 * blocks, LANES), F32),
            pltpu.VMEM((2, blocks, LANES), F32),
            pltpu.VMEM((2, blocks, LANES), jnp.int32),
            pltpu.SMEM((2 * blocks,), jnp.int32),
            pltpu.VMEM((4, blocks, LANES), F32),
            pltpu.VMEM((n * (cap + 1), 1, LANES), F32),
            pltpu.VMEM((n * (cap + 1) + 1, 1, LANES), F32),
            pltpu.VMEM((n * (cap + 1) + 1, 1, LANES), F32),
            pltpu.VMEM((2 * slots, 1, LANES), F32),
            pltpu.VMEM((2 * slots + 2, 1, LANES), F32),
            pltpu.VMEM((n, 1, LANES), jnp.int32),
            pltpu.SMEM((n, 1, LANES), jnp.int32),
            pltpu.VMEM((owners * tcap, 2, cells), F32),
            pltpu.VMEM((owners * tcap, 2, cells), F32),
            pltpu.VMEM((2, blocks, cells), F32),
            pltpu.VMEM((4, blocks, cells), F32),
            dma((2,)),
            dma((2,)),
            dma,
            dma,
            dma,
            dma,
            dma((owners,)),
            dma((owners,)),
            dma,
        ],
        compiler_params=pltpu.CompilerParams(collective_id=0, has_side_effects=True),
    )(plan, row, velocity, stress, ice_mass, strength, coriolis, air_stress, ocean_current)


def solution(mesh):
    split = ("groups", "blk", "sub")
    placed = (
        P(None, split, None),
        P(None, split, None),
        P(split, None),
        P(split, None),
        P(split, None),
        P(None, split, None),
        P(split, None, None),
        P(split, None),
        P(split),
    )
    return jax.shard_map(
        shards,
        mesh=mesh,
        in_specs=placed,
        out_specs=(P(None, split, None), P(None, split, None)),
        check_vma=False,
    )
```

```python
import functools

import jax
import jax.numpy as jnp
from jax import lax
from jax.experimental import pallas as pl
from jax.experimental.pallas import tpu as pltpu
from jax.sharding import PartitionSpec as P

SIDE = 32
SUBCYCLES = 8
LANES = 128
CHUNKS = 8

DELTA_FLOOR = 0.01
RELAX = 0.3
SPEED_FLOOR = 0.01
MESH = pl.DeviceIdType.MESH
F32 = jnp.float32


def roll(x, shift):
    shift = shift % LANES
    return x if shift == 0 else pltpu.roll(x, shift, 1)


def lanes_like(x):
    return lax.broadcasted_iota(jnp.int32, x.shape, 1)


def gather_edges(col_a, col_b, row_a, row_b, col_lane, row_lane):
    lane = lanes_like(row_a)
    inner = lane % SIDE
    quarter = lane // SIDE
    out = jnp.zeros_like(row_a)
    for base, chunks in ((0, col_a), (8, col_b)):
        for k in range(CHUNKS):
            out = jnp.where(inner == base + k, roll(chunks[k], base + k - col_lane), out)
    for base, row in ((16, row_a), (24, row_b)):
        for c in range(4):
            there = (quarter == c) & (inner >= base) & (inner < base + 8)
            out = jnp.where(there, roll(row, 24 * c + base - row_lane), out)
    return out


def column_to(edges, base, k, col_lane):
    return roll(edges, col_lane - base - k)


def row_to(edges, base, row_lane):
    lane = lanes_like(edges)
    out = roll(edges, row_lane - base)
    for c in range(1, 4):
        moved = roll(edges, row_lane - base - 24 * c)
        out = jnp.where(lane >= row_lane + 8 * c, moved, out)
    return out


def chunk(k):
    return pl.ds(LANES * k, LANES)


def repeat(start, stop, body):
    if stop - start <= 64:
        for i in range(start, stop):
            body(i)
    else:

        def step(i, carry):
            body(i)
            return carry

        lax.fori_loop(start, stop, step, 0)


def kernel(
    sizes,
    plan,
    table_row,
    vel_in,
    stress_in,
    mass,
    strength,
    coriolis,
    air,
    ocean,
    vel,
    stress,
    low_edges,
    high_edges,
    near,
    far,
    corners,
    corner_lane,
    corner_slot,
    halo,
    pack,
    recv_even,
    recv_odd,
    h_pack,
    h_recv,
    table,
    table_s,
    ans_pack,
    ans_recv,
    cur,
    consts,
    ready,
    send_sem,
    recv_sem,
    h_send_sem,
    h_recv_sem,
    t_send_sem,
    t_recv_sem,
    a_send_sem,
    a_recv_sem,
    local_sem,
):
    n, owners, cap, tcap, blocks = sizes
    rows = cap + 1
    slots = n * cap
    zero_slot = n * rows
    group, blk, sub = lax.axis_index("groups"), lax.axis_index("blk"), lax.axis_index("sub")
    me = blk * owners + sub
    recv = (recv_even, recv_odd)
    low_src, high_src = 0, slots
    land = 2 * slots
    h_land = land + 4 * blocks
    t_land = h_land + 2 * blocks

    def peer(o):
        d = lax.rem(me + o, n)
        return (group, d // owners, lax.rem(d, owners))

    def sub_peer(o):
        return (group, blk, lax.rem(sub + o + owners, owners))

    def send_to(o, source, target, sent, received, device):
        return pltpu.make_async_remote_copy(
            src_ref=source,
            dst_ref=target,
            send_sem=sent,
            recv_sem=received,
            device_id=device,
            device_id_type=MESH,
        )

    def wait_all(ref, sem):
        pltpu.make_async_copy(ref, ref, sem).wait()

    def answer_copy(o):
        where = pl.ds(o * tcap, tcap)
        return send_to(
            o, ans_pack.at[where], ans_recv.at[where], a_send_sem.at[o], a_recv_sem.at[o], sub_peer(-o)
        )

    barrier = pltpu.get_barrier_semaphore()
    repeat(1, n, lambda o: pl.semaphore_signal(barrier, inc=1, device_id=peer(o), device_id_type=MESH))
    pl.semaphore_wait(barrier, n - 1)
    repeat(
        1, n, lambda o: send_to(o, table_row, table.at[o], t_send_sem, t_recv_sem, peer(o)).start()
    )

    def trade(u, v, parity):
        lane = lanes_like(u[0])
        block = lax.broadcasted_iota(jnp.int32, u[0].shape, 0)
        low = gather_edges(u, v, u[0], v[0], 0, 0)
        high = gather_edges(u, v, u[-1], v[-1], 31, 96)
        low_edges[0:blocks] = low
        low_edges[blocks : 2 * blocks] = roll(low, -16)
        high_edges[0:blocks] = high
        high_edges[blocks : 2 * blocks] = roll(high, 16)
        spread = jnp.zeros_like(low)
        for place, value in enumerate((u[0][:, 31:32], v[0][:, 31:32], u[-1][:, 96:97], v[-1][:, 96:97])):
            spread = jnp.where(lane == block + place * blocks, value, spread)
        corner_row = jnp.sum(spread, axis=0, keepdims=True)
        half = lax.broadcasted_iota(jnp.int32, (1, LANES), 1) % SIDE < 16
        into = recv[parity]

        def fill(o, target):
            for t in range(cap):
                low_row = low_edges[pl.ds(plan[low_src + o * cap + t], 1), :]
                high_row = high_edges[pl.ds(plan[high_src + o * cap + t], 1), :]
                target[o * rows + t] = jnp.where(half, low_row, high_row)
            target[o * rows + cap] = corner_row

        def fill_and_send(o):
            fill(o, pack)
            where = pl.ds(o * rows, rows)
            send_to(
                o, pack.at[where], into.at[where], send_sem.at[parity], recv_sem.at[parity], peer(o)
            ).start()

        repeat(1, n, fill_and_send)
        fill(0, into)

    remote = pl.ds(rows, (n - 1) * rows)

    def arrive(parity):
        wait_all(recv[parity].at[remote], recv_sem.at[parity])
        half = lax.broadcasted_iota(jnp.int32, (1, LANES), 1) % SIDE < 16
        for b in range(blocks):
            east, north, west, south = (recv[parity][plan[land + 4 * b + c]] for c in range(4))
            near[pl.ds(b, 1), :] = jnp.where(half, east, south)
            far[pl.ds(b, 1), :] = jnp.where(half, north, west)
            corners[0, pl.ds(b, 1), :] = recv[parity][corner_slot[b]]
            corners[1, pl.ds(b, 1), :] = recv[parity][corner_slot[blocks + b]]
        straight, crossed = near[0:blocks], far[0:blocks]
        half = lanes_like(straight) % SIDE < 16
        low = jnp.where(half, straight, roll(crossed, 16))
        high = jnp.where(half, roll(crossed, -16), straight)
        return low, high

    def corner_value(which, place):
        x = corners[which]
        hit = lanes_like(x) == corner_lane[which] + place * blocks
        return jnp.sum(jnp.where(hit, x, 0.0), axis=1, keepdims=True)

    def advance(stress_old, u, v, u_e, v_e, u_n, v_n, p):
        along_x, along_y = u_e - u, v_n - v
        diverge = along_x + along_y
        tension = along_x - along_y
        shearing = (u_n - u) + (v_e - v)
        square = diverge * diverge + 0.25 * (tension * tension + shearing * shearing) + DELTA_FLOOR
        viscous = p * lax.rsqrt(square)
        s1, s2, s12 = stress_old
        return (
            s1 + RELAX * (viscous * diverge - p - s1),
            s2 + RELAX * (0.25 * viscous * tension - s2),
            s12 + RELAX * (0.25 * viscous * shearing - s12),
        )

    def halo_step(high):
        lane = lanes_like(high)
        inner = lane % SIDE
        column = inner < 16

        def ahead(x, north_west, south_east):
            up = jnp.where(lane < 96, roll(x, -32), roll(x, 95))
            up = jnp.where(lane == 103, north_west, up)
            right = jnp.where(inner == 23, roll(x, -25), roll(x, -1))
            right = jnp.where(lane == 119, south_east, right)
            return jnp.where(column, up, right)

        mine = low_edges[0:blocks]
        u, v = high, roll(high, -8)
        mine_u, mine_v = mine, roll(mine, -8)
        ahead_u = ahead(u, corner_value(0, 0), corner_value(1, 2))
        ahead_v = ahead(v, corner_value(0, 1), corner_value(1, 3))
        s1, s2, s12 = advance(
            (halo[0], halo[1], halo[2]),
            u,
            v,
            jnp.where(column, mine_u, ahead_u),
            jnp.where(column, mine_v, ahead_v),
            jnp.where(column, ahead_u, mine_u),
            jnp.where(column, ahead_v, mine_v),
            halo[3],
        )
        halo[0], halo[1], halo[2] = s1, s2, s12
        return 0.5 * (s1 + s2), 0.5 * (s1 - s2), 0.5 * s12

    def prepare_shifts(here):
        for c in range(2):
            x = [here[c, :, chunk(k)] for k in range(CHUNKS)]
            moved = [roll(y, -SIDE) for y in x]
            lane = lanes_like(x[0])
            for k in range(CHUNKS):
                ready[4 + c, :, chunk(k)] = roll(x[k], -1)
                north = jnp.where(lane < 96, moved[k], moved[k + 1]) if k + 1 < CHUNKS else moved[k]
                ready[6 + c, :, chunk(k)] = north

    def prepare_drag(here):
        for k in range(CHUNKS):
            u, v = here[0, :, chunk(k)], here[1, :, chunk(k)]
            uo, vo = cur[0, :, chunk(k)], cur[1, :, chunk(k)]
            inertia, r, cx, cy = (consts[c, :, chunk(k)] for c in range(4))
            dx, dy = uo - u, vo - v
            drag = jnp.sqrt(dx * dx + dy * dy + SPEED_FLOOR)
            a = inertia + drag
            inv = 1.0 / (a * a + r * r)
            ready[0, :, chunk(k)] = a * inv
            ready[1, :, chunk(k)] = r * inv
            ready[2, :, chunk(k)] = inertia * u + cx + drag * uo
            ready[3, :, chunk(k)] = inertia * v + cy + drag * vo

    def subcycle(parity, first, last):
        here, old = (vel_in, stress_in) if first else (vel, stress)
        low, high = arrive(parity)
        if first:
            settle_halo()
        halo_xx, halo_yy, halo_xy = halo_step(high)
        lane = lanes_like(low)
        inner = lane % SIDE
        parts = []
        new_u, new_v = [], []

        def stress_chunk(k):
            u, v = here[0, :, chunk(k)], here[1, :, chunk(k)]
            u_n, v_n = ready[6, :, chunk(k)], ready[7, :, chunk(k)]
            if k + 1 == CHUNKS:
                u_n = jnp.where(lane < 96, u_n, row_to(low, 16, 96))
                v_n = jnp.where(lane < 96, v_n, row_to(low, 24, 96))
            s1, s2, s12 = advance(
                [old[c, :, chunk(k)] for c in range(3)],
                u,
                v,
                jnp.where(inner == 31, column_to(low, 0, k, 31), ready[4, :, chunk(k)]),
                jnp.where(inner == 31, column_to(low, 8, k, 31), ready[5, :, chunk(k)]),
                u_n,
                v_n,
                strength[:, chunk(k)],
            )
            stress[0, :, chunk(k)] = s1
            stress[1, :, chunk(k)] = s2
            stress[2, :, chunk(k)] = s12
            xx, yy, xy = 0.5 * (s1 + s2), 0.5 * (s1 - s2), 0.5 * s12
            parts.append((xx, yy, xy, roll(yy, SIDE), roll(xy, SIDE)))

        def velocity_chunk(k):
            xx, yy, xy, moved_yy, moved_xy = parts[k]
            if k:
                before_yy, before_xy = parts[k - 1][3:]
            else:
                before_yy, before_xy = row_to(halo_yy, 16, 0), row_to(halo_xy, 16, 0)
            xx_w = jnp.where(inner == 0, column_to(halo_xx, 0, k, 0), roll(xx, 1))
            xy_w = jnp.where(inner == 0, column_to(halo_xy, 0, k, 0), roll(xy, 1))
            yy_s = jnp.where(lane < SIDE, before_yy, moved_yy)
            xy_s = jnp.where(lane < SIDE, before_xy, moved_xy)
            a, r, gx, gy = (ready[c, :, chunk(k)] for c in range(4))
            gx = gx + (xx - xx_w + xy - xy_s)
            gy = gy + (xy - xy_w + yy - yy_s)
            u, v = a * gx + r * gy, a * gy - r * gx
            vel[0, :, chunk(k)] = u
            vel[1, :, chunk(k)] = v
            new_u.append(u)
            new_v.append(v)

        if first:
            for k in range(CHUNKS):
                stress_chunk(k)
            settle_ocean()
            prepare_drag(here)
            for k in range(CHUNKS):
                velocity_chunk(k)
        else:
            for k in range(CHUNKS):
                stress_chunk(k)
                velocity_chunk(k)
        wait_all(pack.at[remote], send_sem.at[parity])
        if not last:
            trade(new_u, new_v, 1 - parity)
            prepare_shifts(vel)
            prepare_drag(vel)

    def settle_halo():
        wait_all(h_recv.at[pl.ds(2 * cap, 2 * (slots - cap))], h_recv_sem)
        wait_all(h_pack.at[pl.ds(2 * cap, 2 * (slots - cap))], h_send_sem)
        half = lax.broadcasted_iota(jnp.int32, (1, LANES), 1) % SIDE < 16
        for b in range(blocks):
            west, south = 2 * plan[h_land + 2 * b], 2 * plan[h_land + 2 * b + 1]
            near[pl.ds(b, 1), :] = jnp.where(half, h_recv[west], h_recv[south])
            far[pl.ds(b, 1), :] = jnp.where(half, h_recv[west + 1], h_recv[south + 1])
        first, second = near[0:blocks], far[0:blocks]
        halo[0], halo[1] = first, roll(first, -8)
        halo[2], halo[3] = second, roll(second, -8)

    def settle_ocean():
        for o in range(1, owners):
            answer_copy(o).wait()
        for b in range(blocks):
            row = ans_recv[plan[t_land + b]]
            cur[0, pl.ds(b, 1), :] = row[0:1]
            cur[1, pl.ds(b, 1), :] = row[1:2]
        for k in range(CHUNKS):
            m = mass[:, chunk(k)]
            r = m * coriolis[:, chunk(k)]
            consts[0, :, chunk(k)] = 2.0 * m
            consts[1, :, chunk(k)] = r
            consts[2, :, chunk(k)] = air[0, :, chunk(k)] - r * cur[1, :, chunk(k)]
            consts[3, :, chunk(k)] = air[1, :, chunk(k)] + r * cur[0, :, chunk(k)]

    zero_row = jnp.zeros((1, LANES), F32)
    recv_even[zero_slot] = zero_row
    recv_odd[zero_slot] = zero_row
    h_recv[2 * slots] = zero_row
    h_recv[2 * slots + 1] = zero_row
    trade([vel_in[0, :, chunk(k)] for k in range(CHUNKS)], [vel_in[1, :, chunk(k)] for k in range(CHUNKS)], 0)

    table[0] = table_row[...]
    wait_all(table.at[pl.ds(1, n - 1)], t_recv_sem)
    wait_all(table.at[pl.ds(1, n - 1)], t_send_sem)
    to_scalar = pltpu.make_async_copy(table, table_s, local_sem)
    to_scalar.start()
    to_scalar.wait()
    for o in range(owners):
        holder = blk * owners + lax.rem(sub - o + owners, owners)
        slot = lax.rem(me - holder + n, n)
        for t in range(tcap):
            tile = ocean[table_s[slot, 0, 4 * blocks + o * tcap + t]]
            (ans_pack if o else ans_recv)[o * tcap + t] = tile
        if o:
            answer_copy(o).start()
    s1, s2, s12 = ([stress_in[c, :, chunk(k)] for k in range(CHUNKS)] for c in range(3))
    p = [strength[:, chunk(k)] for k in range(CHUNKS)]
    first = gather_edges(s1, s2, s1[-1], s2[-1], 31, 96)
    second = gather_edges(s12, p, s12[-1], p[-1], 31, 96)
    for copy in range(2):
        near[copy * blocks : (copy + 1) * blocks] = first
        far[copy * blocks : (copy + 1) * blocks] = second

    def fill_halo(o, target):
        for t in range(cap):
            s = plan[high_src + o * cap + t]
            target[2 * (o * cap + t)] = near[pl.ds(s, 1), :]
            target[2 * (o * cap + t) + 1] = far[pl.ds(s, 1), :]

    def send_halo(o):
        fill_halo(o, h_pack)
        where = pl.ds(2 * o * cap, 2 * cap)
        send_to(o, h_pack.at[where], h_recv.at[where], h_send_sem, h_recv_sem, peer(o)).start()

    repeat(1, n, send_halo)
    fill_halo(0, h_recv)

    for b in range(blocks):
        for which in range(2):
            via = jnp.maximum(table_s[0, 0, 4 * b + which], 0)
            there = lax.rem(me - via // blocks + n, n)
            far_block = table_s[there, 0, 4 * lax.rem(via, blocks) + 3 - which]
            known = far_block >= 0
            far_block = jnp.maximum(far_block, 0)
            slot = lax.rem(me - far_block // blocks + n, n) * rows + cap
            corner_slot[which * blocks + b] = jnp.where(known, slot, zero_slot)
            corner_lane[which, pl.ds(b, 1), :] = jnp.full((1, LANES), lax.rem(far_block, blocks), jnp.int32)

    prepare_shifts(vel_in)
    subcycle(0, True, False)

    def pair(_, carry):
        subcycle(1, False, False)
        subcycle(0, False, False)
        return carry

    lax.fori_loop(0, (SUBCYCLES - 2) // 2, pair, 0)
    subcycle(1, False, True)


def make_plan(neighbours, ocean_tile, sizes, tiles_dev):
    n, owners, cap, tcap, blocks = sizes
    sub = lax.axis_index("sub")
    me = lax.axis_index("blk") * owners + sub
    entry = jnp.arange(2 * blocks, dtype=jnp.int32)

    def sending(targets, content):
        t = targets.reshape(-1)
        away = jnp.where(t >= 0, (t // blocks - me) % n, n)
        ahead = (away[:, None] == away[None, :]) & (entry[None, :] < entry[:, None])
        place = away * cap + jnp.sum(ahead.astype(jnp.int32), axis=1)
        slot = jnp.arange(n * cap, dtype=jnp.int32)
        hit = (place[None, :] == slot[:, None]) & (away < n)[None, :]
        return jnp.sum(jnp.where(hit, content[None, :], 0), axis=1)

    def landing(sources):
        s = sources.reshape(-1)
        known = s >= 0
        away = jnp.where(known, (me - s // blocks) % n, n)
        key = s * 2 + entry % 2
        ahead = (away[:, None] == away[None, :]) & (key[None, :] < key[:, None])
        rank = jnp.sum(ahead.astype(jnp.int32), axis=1)
        main = jnp.where(known, away * (cap + 1) + rank, n * (cap + 1))
        return main.reshape(-1, 2), jnp.where(known, away * cap + rank, n * cap)

    away = (ocean_tile // tiles_dev - sub) % owners
    order = jnp.arange(blocks, dtype=jnp.int32)
    ahead = (away[:, None] == away[None, :]) & (order[None, :] < order[:, None])
    place = away * tcap + jnp.sum(ahead.astype(jnp.int32), axis=1)
    hit = jnp.arange(owners * tcap, dtype=jnp.int32)[:, None] == place[None, :]
    requests = jnp.sum(jnp.where(hit, (ocean_tile % tiles_dev)[None, :], 0), axis=1)
    row = jnp.concatenate([neighbours.reshape(-1), requests])
    row = jnp.pad(row, (0, LANES - row.shape[0])).reshape(1, LANES)
    from_east, _ = landing(neighbours[:, 2:4])
    from_west, halo_land = landing(neighbours[:, 0:2])
    kind = entry % 2
    plan = jnp.concatenate(
        [
            sending(neighbours[:, 0:2], entry // 2 + kind * blocks),
            sending(neighbours[:, 2:4], entry // 2 + (1 - kind) * blocks),
            jnp.concatenate([from_east, from_west], axis=1).reshape(-1),
            halo_land,
            place,
        ]
    )
    return plan, row


def shards(
    velocity, stress, ice_mass, strength, coriolis, air_stress, ocean_current, neighbours, ocean_tile
):
    blocks = velocity.shape[1]
    n = lax.axis_size(("blk", "sub"))
    owners = lax.axis_size("sub")
    cap = max(2, 4 * blocks // n)
    tcap = max(1, 2 * blocks // owners)
    sizes = (n, owners, cap, tcap, blocks)
    cells = velocity.shape[2]
    plan, row = make_plan(neighbours, ocean_tile, sizes, ocean_current.shape[0])
    slots = n * cap
    vmem = pl.BlockSpec(memory_space=pltpu.VMEM)
    dma = pltpu.SemaphoreType.DMA
    return pl.pallas_call(
        functools.partial(kernel, sizes),
        out_shape=(
            jax.ShapeDtypeStruct(velocity.shape, F32),
            jax.ShapeDtypeStruct(stress.shape, F32),
        ),
        in_specs=[pl.BlockSpec(memory_space=pltpu.SMEM)] + [vmem] * 8,
        out_specs=(vmem, vmem),
        scratch_shapes=[
            pltpu.VMEM((2 * blocks, LANES), F32),
            pltpu.VMEM((2 * blocks, LANES), F32),
            pltpu.VMEM((2 * blocks, LANES), F32),
            pltpu.VMEM((2 * blocks, LANES), F32),
            pltpu.VMEM((2, blocks, LANES), F32),
            pltpu.VMEM((2, blocks, LANES), jnp.int32),
            pltpu.SMEM((2 * blocks,), jnp.int32),
            pltpu.VMEM((4, blocks, LANES), F32),
            pltpu.VMEM((n * (cap + 1), 1, LANES), F32),
            pltpu.VMEM((n * (cap + 1) + 1, 1, LANES), F32),
            pltpu.VMEM((n * (cap + 1) + 1, 1, LANES), F32),
            pltpu.VMEM((2 * slots, 1, LANES), F32),
            pltpu.VMEM((2 * slots + 2, 1, LANES), F32),
            pltpu.VMEM((n, 1, LANES), jnp.int32),
            pltpu.SMEM((n, 1, LANES), jnp.int32),
            pltpu.VMEM((owners * tcap, 2, cells), F32),
            pltpu.VMEM((owners * tcap, 2, cells), F32),
            pltpu.VMEM((2, blocks, cells), F32),
            pltpu.VMEM((4, blocks, cells), F32),
            pltpu.VMEM((8, blocks, cells), F32),
            dma((2,)),
            dma((2,)),
            dma,
            dma,
            dma,
            dma,
            dma((owners,)),
            dma((owners,)),
            dma,
        ],
        compiler_params=pltpu.CompilerParams(collective_id=0, has_side_effects=True),
    )(plan, row, velocity, stress, ice_mass, strength, coriolis, air_stress, ocean_current)


def solution(mesh):
    split = ("groups", "blk", "sub")
    placed = (
        P(None, split, None),
        P(None, split, None),
        P(split, None),
        P(split, None),
        P(split, None),
        P(None, split, None),
        P(split, None, None),
        P(split, None),
        P(split),
    )
    return jax.shard_map(
        shards,
        mesh=mesh,
        in_specs=placed,
        out_specs=(P(None, split, None), P(None, split, None)),
        check_vma=False,
    )
```

```python
import functools

import jax
import jax.numpy as jnp
from jax import lax
from jax.experimental import pallas as pl
from jax.experimental.pallas import tpu as pltpu
from jax.sharding import PartitionSpec as P

SIDE = 32
SUBCYCLES = 8
LANES = 128
CHUNKS = 8

DELTA_FLOOR = 0.01
RELAX = 0.3
SPEED_FLOOR = 0.01
MESH = pl.DeviceIdType.MESH
F32 = jnp.float32


def roll(x, shift):
    shift = shift % LANES
    return x if shift == 0 else pltpu.roll(x, shift, 1)


def lanes_like(x):
    return lax.broadcasted_iota(jnp.int32, x.shape, 1)


def gather_edges(col_a, col_b, row_a, row_b, col_lane, row_lane):
    lane = lanes_like(row_a)
    inner = lane % SIDE
    quarter = lane // SIDE
    out = jnp.zeros_like(row_a)
    for base, chunks in ((0, col_a), (8, col_b)):
        for k in range(CHUNKS):
            out = jnp.where(inner == base + k, roll(chunks[k], base + k - col_lane), out)
    for base, row in ((16, row_a), (24, row_b)):
        for c in range(4):
            there = (quarter == c) & (inner >= base) & (inner < base + 8)
            out = jnp.where(there, roll(row, 24 * c + base - row_lane), out)
    return out


def column_to(edges, base, k, col_lane):
    return roll(edges, col_lane - base - k)


def row_to(edges, base, row_lane):
    lane = lanes_like(edges)
    out = roll(edges, row_lane - base)
    for c in range(1, 4):
        moved = roll(edges, row_lane - base - 24 * c)
        out = jnp.where(lane >= row_lane + 8 * c, moved, out)
    return out


def chunk(k):
    return pl.ds(LANES * k, LANES)


def repeat(start, stop, body):
    if stop - start <= 64:
        for i in range(start, stop):
            body(i)
    else:

        def step(i, carry):
            body(i)
            return carry

        lax.fori_loop(start, stop, step, 0)


def kernel(
    sizes,
    plan,
    table_row,
    vel_in,
    stress_in,
    mass,
    strength,
    coriolis,
    air,
    ocean,
    vel,
    stress,
    low_edges,
    high_edges,
    near,
    far,
    corners,
    corner_lane,
    corner_slot,
    halo,
    pack,
    recv_even,
    recv_odd,
    h_pack,
    h_recv,
    table,
    table_s,
    ans_pack,
    ans_recv,
    cur,
    consts,
    ready,
    send_sem,
    recv_sem,
    h_send_sem,
    h_recv_sem,
    t_send_sem,
    t_recv_sem,
    a_send_sem,
    a_recv_sem,
    local_sem,
):
    n, owners, cap, tcap, blocks = sizes
    rows = cap + 1
    slots = n * cap
    zero_slot = n * rows
    group, blk, sub = lax.axis_index("groups"), lax.axis_index("blk"), lax.axis_index("sub")
    me = blk * owners + sub
    recv = (recv_even, recv_odd)
    low_src, high_src = 0, slots
    land = 2 * slots
    h_land = land + 4 * blocks
    t_land = h_land + 2 * blocks

    def peer(o):
        d = lax.rem(me + o, n)
        return (group, d // owners, lax.rem(d, owners))

    def sub_peer(o):
        return (group, blk, lax.rem(sub + o + owners, owners))

    def send_to(o, source, target, sent, received, device):
        return pltpu.make_async_remote_copy(
            src_ref=source,
            dst_ref=target,
            send_sem=sent,
            recv_sem=received,
            device_id=device,
            device_id_type=MESH,
        )

    def wait_all(ref, sem):
        pltpu.make_async_copy(ref, ref, sem).wait()

    def answer_copy(o):
        where = pl.ds(o * tcap, tcap)
        return send_to(
            o, ans_pack.at[where], ans_recv.at[where], a_send_sem.at[o], a_recv_sem.at[o], sub_peer(-o)
        )

    barrier = pltpu.get_barrier_semaphore()
    repeat(1, n, lambda o: pl.semaphore_signal(barrier, inc=1, device_id=peer(o), device_id_type=MESH))
    pl.semaphore_wait(barrier, n - 1)
    repeat(
        1, n, lambda o: send_to(o, table_row, table.at[o], t_send_sem, t_recv_sem, peer(o)).start()
    )

    def trade(u, v, parity):
        lane = lanes_like(u[0])
        block = lax.broadcasted_iota(jnp.int32, u[0].shape, 0)
        low = gather_edges(u, v, u[0], v[0], 0, 0)
        high = gather_edges(u, v, u[-1], v[-1], 31, 96)
        low_edges[0:blocks] = low
        low_edges[blocks : 2 * blocks] = roll(low, -16)
        high_edges[0:blocks] = high
        high_edges[blocks : 2 * blocks] = roll(high, 16)
        spread = jnp.zeros_like(low)
        for place, value in enumerate((u[0][:, 31:32], v[0][:, 31:32], u[-1][:, 96:97], v[-1][:, 96:97])):
            spread = jnp.where(lane == block + place * blocks, value, spread)
        corner_row = jnp.sum(spread, axis=0, keepdims=True)
        half = lax.broadcasted_iota(jnp.int32, (1, LANES), 1) % SIDE < 16
        into = recv[parity]

        def fill(o, target):
            for t in range(cap):
                low_row = low_edges[pl.ds(plan[low_src + o * cap + t], 1), :]
                high_row = high_edges[pl.ds(plan[high_src + o * cap + t], 1), :]
                target[o * rows + t] = jnp.where(half, low_row, high_row)
            target[o * rows + cap] = corner_row

        def fill_and_send(o):
            fill(o, pack)
            where = pl.ds(o * rows, rows)
            send_to(
                o, pack.at[where], into.at[where], send_sem.at[parity], recv_sem.at[parity], peer(o)
            ).start()

        repeat(1, n, fill_and_send)
        fill(0, into)

    remote = pl.ds(rows, (n - 1) * rows)

    def arrive(parity):
        wait_all(recv[parity].at[remote], recv_sem.at[parity])
        half = lax.broadcasted_iota(jnp.int32, (1, LANES), 1) % SIDE < 16
        for b in range(blocks):
            east, north, west, south = (recv[parity][plan[land + 4 * b + c]] for c in range(4))
            near[pl.ds(b, 1), :] = jnp.where(half, east, south)
            far[pl.ds(b, 1), :] = jnp.where(half, north, west)
            corners[0, pl.ds(b, 1), :] = recv[parity][corner_slot[b]]
            corners[1, pl.ds(b, 1), :] = recv[parity][corner_slot[blocks + b]]
        straight, crossed = near[0:blocks], far[0:blocks]
        half = lanes_like(straight) % SIDE < 16
        low = jnp.where(half, straight, roll(crossed, 16))
        high = jnp.where(half, roll(crossed, -16), straight)
        return low, high

    def corner_value(which, place):
        x = corners[which]
        hit = lanes_like(x) == corner_lane[which] + place * blocks
        return jnp.sum(jnp.where(hit, x, 0.0), axis=1, keepdims=True)

    def advance(stress_old, u, v, u_e, v_e, u_n, v_n, p):
        along_x, along_y = u_e - u, v_n - v
        diverge = along_x + along_y
        tension = along_x - along_y
        shearing = (u_n - u) + (v_e - v)
        square = diverge * diverge + 0.25 * (tension * tension + shearing * shearing) + DELTA_FLOOR
        viscous = p * lax.rsqrt(square)
        s1, s2, s12 = stress_old
        return (
            s1 + RELAX * (viscous * diverge - p - s1),
            s2 + RELAX * (0.25 * viscous * tension - s2),
            s12 + RELAX * (0.25 * viscous * shearing - s12),
        )

    def halo_step(high):
        lane = lanes_like(high)
        inner = lane % SIDE
        column = inner < 16

        def ahead(x, north_west, south_east):
            up = jnp.where(lane < 96, roll(x, -32), roll(x, 95))
            up = jnp.where(lane == 103, north_west, up)
            right = jnp.where(inner == 23, roll(x, -25), roll(x, -1))
            right = jnp.where(lane == 119, south_east, right)
            return jnp.where(column, up, right)

        mine = low_edges[0:blocks]
        u, v = high, roll(high, -8)
        mine_u, mine_v = mine, roll(mine, -8)
        ahead_u = ahead(u, corner_value(0, 0), corner_value(1, 2))
        ahead_v = ahead(v, corner_value(0, 1), corner_value(1, 3))
        s1, s2, s12 = advance(
            (halo[0], halo[1], halo[2]),
            u,
            v,
            jnp.where(column, mine_u, ahead_u),
            jnp.where(column, mine_v, ahead_v),
            jnp.where(column, ahead_u, mine_u),
            jnp.where(column, ahead_v, mine_v),
            halo[3],
        )
        halo[0], halo[1], halo[2] = s1, s2, s12
        return 0.5 * (s1 + s2), 0.5 * (s1 - s2), 0.5 * s12

    def prepare_shifts(here):
        for c in range(2):
            x = [here[c, :, chunk(k)] for k in range(CHUNKS)]
            moved = [roll(y, -SIDE) for y in x]
            lane = lanes_like(x[0])
            for k in range(CHUNKS):
                ready[4 + c, :, chunk(k)] = roll(x[k], -1)
                north = jnp.where(lane < 96, moved[k], moved[k + 1]) if k + 1 < CHUNKS else moved[k]
                ready[6 + c, :, chunk(k)] = north

    def prepare_drag(here):
        for k in range(CHUNKS):
            u, v = here[0, :, chunk(k)], here[1, :, chunk(k)]
            uo, vo = cur[0, :, chunk(k)], cur[1, :, chunk(k)]
            inertia, r, cx, cy = (consts[c, :, chunk(k)] for c in range(4))
            dx, dy = uo - u, vo - v
            drag = jnp.sqrt(dx * dx + dy * dy + SPEED_FLOOR)
            a = inertia + drag
            inv = 1.0 / (a * a + r * r)
            ready[0, :, chunk(k)] = a * inv
            ready[1, :, chunk(k)] = r * inv
            ready[2, :, chunk(k)] = inertia * u + cx + drag * uo
            ready[3, :, chunk(k)] = inertia * v + cy + drag * vo

    def subcycle(parity, first, last):
        here, old = (vel_in, stress_in) if first else (vel, stress)
        low, high = arrive(parity)
        if first:
            settle_halo()
        halo_xx, halo_yy, halo_xy = halo_step(high)
        lane = lanes_like(low)
        inner = lane % SIDE
        parts = []
        new_u, new_v = [], []

        def stress_chunk(k):
            u, v = here[0, :, chunk(k)], here[1, :, chunk(k)]
            u_n, v_n = ready[6, :, chunk(k)], ready[7, :, chunk(k)]
            if k + 1 == CHUNKS:
                u_n = jnp.where(lane < 96, u_n, row_to(low, 16, 96))
                v_n = jnp.where(lane < 96, v_n, row_to(low, 24, 96))
            s1, s2, s12 = advance(
                [old[c, :, chunk(k)] for c in range(3)],
                u,
                v,
                jnp.where(inner == 31, column_to(low, 0, k, 31), ready[4, :, chunk(k)]),
                jnp.where(inner == 31, column_to(low, 8, k, 31), ready[5, :, chunk(k)]),
                u_n,
                v_n,
                strength[:, chunk(k)],
            )
            stress[0, :, chunk(k)] = s1
            stress[1, :, chunk(k)] = s2
            stress[2, :, chunk(k)] = s12
            xx, yy, xy = 0.5 * (s1 + s2), 0.5 * (s1 - s2), 0.5 * s12
            parts.append((xx, yy, xy, roll(yy, SIDE), roll(xy, SIDE)))

        def velocity_chunk(k):
            xx, yy, xy, moved_yy, moved_xy = parts[k]
            if k:
                before_yy, before_xy = parts[k - 1][3:]
            else:
                before_yy, before_xy = row_to(halo_yy, 16, 0), row_to(halo_xy, 16, 0)
            xx_w = jnp.where(inner == 0, column_to(halo_xx, 0, k, 0), roll(xx, 1))
            xy_w = jnp.where(inner == 0, column_to(halo_xy, 0, k, 0), roll(xy, 1))
            yy_s = jnp.where(lane < SIDE, before_yy, moved_yy)
            xy_s = jnp.where(lane < SIDE, before_xy, moved_xy)
            a, r, gx, gy = (ready[c, :, chunk(k)] for c in range(4))
            gx = gx + (xx - xx_w + xy - xy_s)
            gy = gy + (xy - xy_w + yy - yy_s)
            u, v = a * gx + r * gy, a * gy - r * gx
            vel[0, :, chunk(k)] = u
            vel[1, :, chunk(k)] = v
            new_u.append(u)
            new_v.append(v)

        if first:
            for k in range(CHUNKS):
                stress_chunk(k)
            settle_ocean()
            prepare_drag(here)
            for k in range(CHUNKS):
                velocity_chunk(k)
        else:
            for k in range(CHUNKS):
                stress_chunk(k)
                velocity_chunk(k)
        wait_all(pack.at[remote], send_sem.at[parity])
        if not last:
            trade(new_u, new_v, 1 - parity)
            prepare_shifts(vel)
            prepare_drag(vel)

    def settle_halo():
        wait_all(h_recv.at[pl.ds(2 * cap, 2 * (slots - cap))], h_recv_sem)
        wait_all(h_pack.at[pl.ds(2 * cap, 2 * (slots - cap))], h_send_sem)
        half = lax.broadcasted_iota(jnp.int32, (1, LANES), 1) % SIDE < 16
        for b in range(blocks):
            west, south = 2 * plan[h_land + 2 * b], 2 * plan[h_land + 2 * b + 1]
            near[pl.ds(b, 1), :] = jnp.where(half, h_recv[west], h_recv[south])
            far[pl.ds(b, 1), :] = jnp.where(half, h_recv[west + 1], h_recv[south + 1])
        first, second = near[0:blocks], far[0:blocks]
        halo[0], halo[1] = first, roll(first, -8)
        halo[2], halo[3] = second, roll(second, -8)

    def settle_ocean():
        for o in range(1, owners):
            answer_copy(o).wait()
        for b in range(blocks):
            row = ans_recv[plan[t_land + b]]
            cur[0, pl.ds(b, 1), :] = row[0:1]
            cur[1, pl.ds(b, 1), :] = row[1:2]
        for k in range(CHUNKS):
            m = mass[:, chunk(k)]
            r = m * coriolis[:, chunk(k)]
            consts[0, :, chunk(k)] = 2.0 * m
            consts[1, :, chunk(k)] = r
            consts[2, :, chunk(k)] = air[0, :, chunk(k)] - r * cur[1, :, chunk(k)]
            consts[3, :, chunk(k)] = air[1, :, chunk(k)] + r * cur[0, :, chunk(k)]

    zero_row = jnp.zeros((1, LANES), F32)
    recv_even[zero_slot] = zero_row
    recv_odd[zero_slot] = zero_row
    h_recv[2 * slots] = zero_row
    h_recv[2 * slots + 1] = zero_row
    trade([vel_in[0, :, chunk(k)] for k in range(CHUNKS)], [vel_in[1, :, chunk(k)] for k in range(CHUNKS)], 0)

    s1, s2, s12 = ([stress_in[c, :, chunk(k)] for k in range(CHUNKS)] for c in range(3))
    p = [strength[:, chunk(k)] for k in range(CHUNKS)]
    first = gather_edges(s1, s2, s1[-1], s2[-1], 31, 96)
    second = gather_edges(s12, p, s12[-1], p[-1], 31, 96)
    for copy in range(2):
        near[copy * blocks : (copy + 1) * blocks] = first
        far[copy * blocks : (copy + 1) * blocks] = second

    def fill_halo(o, target):
        for t in range(cap):
            s = plan[high_src + o * cap + t]
            target[2 * (o * cap + t)] = near[pl.ds(s, 1), :]
            target[2 * (o * cap + t) + 1] = far[pl.ds(s, 1), :]

    def send_halo(o):
        fill_halo(o, h_pack)
        where = pl.ds(2 * o * cap, 2 * cap)
        send_to(o, h_pack.at[where], h_recv.at[where], h_send_sem, h_recv_sem, peer(o)).start()

    repeat(1, n, send_halo)
    fill_halo(0, h_recv)

    table[0] = table_row[...]
    wait_all(table.at[pl.ds(1, n - 1)], t_recv_sem)
    wait_all(table.at[pl.ds(1, n - 1)], t_send_sem)
    to_scalar = pltpu.make_async_copy(table, table_s, local_sem)
    to_scalar.start()
    to_scalar.wait()
    for o in range(owners):
        holder = blk * owners + lax.rem(sub - o + owners, owners)
        slot = lax.rem(me - holder + n, n)
        for t in range(tcap):
            tile = ocean[table_s[slot, 0, 4 * blocks + o * tcap + t]]
            (ans_pack if o else ans_recv)[o * tcap + t] = tile
        if o:
            answer_copy(o).start()
    for b in range(blocks):
        for which in range(2):
            via = jnp.maximum(table_s[0, 0, 4 * b + which], 0)
            there = lax.rem(me - via // blocks + n, n)
            far_block = table_s[there, 0, 4 * lax.rem(via, blocks) + 3 - which]
            known = far_block >= 0
            far_block = jnp.maximum(far_block, 0)
            slot = lax.rem(me - far_block // blocks + n, n) * rows + cap
            corner_slot[which * blocks + b] = jnp.where(known, slot, zero_slot)
            corner_lane[which, pl.ds(b, 1), :] = jnp.full((1, LANES), lax.rem(far_block, blocks), jnp.int32)

    prepare_shifts(vel_in)
    subcycle(0, True, False)

    def pair(_, carry):
        subcycle(1, False, False)
        subcycle(0, False, False)
        return carry

    lax.fori_loop(0, (SUBCYCLES - 2) // 2, pair, 0)
    subcycle(1, False, True)


def make_plan(neighbours, ocean_tile, sizes, tiles_dev):
    n, owners, cap, tcap, blocks = sizes
    sub = lax.axis_index("sub")
    me = lax.axis_index("blk") * owners + sub
    entry = jnp.arange(2 * blocks, dtype=jnp.int32)

    def sending(targets, content):
        t = targets.reshape(-1)
        away = jnp.where(t >= 0, (t // blocks - me) % n, n)
        ahead = (away[:, None] == away[None, :]) & (entry[None, :] < entry[:, None])
        place = away * cap + jnp.sum(ahead.astype(jnp.int32), axis=1)
        slot = jnp.arange(n * cap, dtype=jnp.int32)
        hit = (place[None, :] == slot[:, None]) & (away < n)[None, :]
        return jnp.sum(jnp.where(hit, content[None, :], 0), axis=1)

    def landing(sources):
        s = sources.reshape(-1)
        known = s >= 0
        away = jnp.where(known, (me - s // blocks) % n, n)
        key = s * 2 + entry % 2
        ahead = (away[:, None] == away[None, :]) & (key[None, :] < key[:, None])
        rank = jnp.sum(ahead.astype(jnp.int32), axis=1)
        main = jnp.where(known, away * (cap + 1) + rank, n * (cap + 1))
        return main.reshape(-1, 2), jnp.where(known, away * cap + rank, n * cap)

    away = (ocean_tile // tiles_dev - sub) % owners
    order = jnp.arange(blocks, dtype=jnp.int32)
    ahead = (away[:, None] == away[None, :]) & (order[None, :] < order[:, None])
    place = away * tcap + jnp.sum(ahead.astype(jnp.int32), axis=1)
    hit = jnp.arange(owners * tcap, dtype=jnp.int32)[:, None] == place[None, :]
    requests = jnp.sum(jnp.where(hit, (ocean_tile % tiles_dev)[None, :], 0), axis=1)
    row = jnp.concatenate([neighbours.reshape(-1), requests])
    row = jnp.pad(row, (0, LANES - row.shape[0])).reshape(1, LANES)
    from_east, _ = landing(neighbours[:, 2:4])
    from_west, halo_land = landing(neighbours[:, 0:2])
    kind = entry % 2
    plan = jnp.concatenate(
        [
            sending(neighbours[:, 0:2], entry // 2 + kind * blocks),
            sending(neighbours[:, 2:4], entry // 2 + (1 - kind) * blocks),
            jnp.concatenate([from_east, from_west], axis=1).reshape(-1),
            halo_land,
            place,
        ]
    )
    return plan, row


def shards(
    velocity, stress, ice_mass, strength, coriolis, air_stress, ocean_current, neighbours, ocean_tile
):
    blocks = velocity.shape[1]
    n = lax.axis_size(("blk", "sub"))
    owners = lax.axis_size("sub")
    cap = max(2, 4 * blocks // n)
    tcap = max(1, 2 * blocks // owners)
    sizes = (n, owners, cap, tcap, blocks)
    cells = velocity.shape[2]
    plan, row = make_plan(neighbours, ocean_tile, sizes, ocean_current.shape[0])
    slots = n * cap
    vmem = pl.BlockSpec(memory_space=pltpu.VMEM)
    dma = pltpu.SemaphoreType.DMA
    return pl.pallas_call(
        functools.partial(kernel, sizes),
        out_shape=(
            jax.ShapeDtypeStruct(velocity.shape, F32),
            jax.ShapeDtypeStruct(stress.shape, F32),
        ),
        in_specs=[pl.BlockSpec(memory_space=pltpu.SMEM)] + [vmem] * 8,
        out_specs=(vmem, vmem),
        scratch_shapes=[
            pltpu.VMEM((2 * blocks, LANES), F32),
            pltpu.VMEM((2 * blocks, LANES), F32),
            pltpu.VMEM((2 * blocks, LANES), F32),
            pltpu.VMEM((2 * blocks, LANES), F32),
            pltpu.VMEM((2, blocks, LANES), F32),
            pltpu.VMEM((2, blocks, LANES), jnp.int32),
            pltpu.SMEM((2 * blocks,), jnp.int32),
            pltpu.VMEM((4, blocks, LANES), F32),
            pltpu.VMEM((n * (cap + 1), 1, LANES), F32),
            pltpu.VMEM((n * (cap + 1) + 1, 1, LANES), F32),
            pltpu.VMEM((n * (cap + 1) + 1, 1, LANES), F32),
            pltpu.VMEM((2 * slots, 1, LANES), F32),
            pltpu.VMEM((2 * slots + 2, 1, LANES), F32),
            pltpu.VMEM((n, 1, LANES), jnp.int32),
            pltpu.SMEM((n, 1, LANES), jnp.int32),
            pltpu.VMEM((owners * tcap, 2, cells), F32),
            pltpu.VMEM((owners * tcap, 2, cells), F32),
            pltpu.VMEM((2, blocks, cells), F32),
            pltpu.VMEM((4, blocks, cells), F32),
            pltpu.VMEM((8, blocks, cells), F32),
            dma((2,)),
            dma((2,)),
            dma,
            dma,
            dma,
            dma,
            dma((owners,)),
            dma((owners,)),
            dma,
        ],
        compiler_params=pltpu.CompilerParams(collective_id=0, has_side_effects=True),
    )(plan, row, velocity, stress, ice_mass, strength, coriolis, air_stress, ocean_current)


def solution(mesh):
    split = ("groups", "blk", "sub")
    placed = (
        P(None, split, None),
        P(None, split, None),
        P(split, None),
        P(split, None),
        P(split, None),
        P(None, split, None),
        P(split, None, None),
        P(split, None),
        P(split),
    )
    return jax.shard_map(
        shards,
        mesh=mesh,
        in_specs=placed,
        out_specs=(P(None, split, None), P(None, split, None)),
        check_vma=False,
    )
```
